128 devices in a mesh: row: 32 (over x, z, y_hi), col: 4 (over y_lo, core).
Axes of the slice: x: 4, y: 4 (y_hi: 2, y_lo: 2; y = y_hi * 2 + y_lo), z: 4, core: 2. Of those that a mesh axis runs over, the one named last changes fastest.
Arguments:
- counts: int32 [3, 32768, 4096], P(None, 'row', 'col'), may hold values from 0 to 255, as said below
- row_embed: float32 [32768, 256], P('row'), may hold values from -1.5 to 1.5
- row_accum: float32 [32768, 256], P('row'), may hold values from 0.5 to 4
- col_embed: float32 [4096, 256], P('col'), may hold values from -1.5 to 1.5
- col_accum: float32 [4096, 256], P('col'), may hold values from 0.5 to 4
- row_log: float32 [32768], P('row'), may hold values from -4 to 4
- col_log: float32 [4096], P('col'), may hold values from -4 to 4
Outputs:
- row_embed_out: float32 [32768, 256], P('row')
- row_accum_out: float32 [32768, 256], P('row')
- col_embed_out: float32 [4096, 256], P('col')
- col_accum_out: float32 [4096, 256], P('col')
The draws below stay inside these ranges and needn't reach their ends.
Inputs may be any that keep to these rules, and one draw needn't show every extreme that they name: About a third of the counts are zero; 255 is reached.
All inputs are finite; a program needn't handle non-finite values.
Results may differ from the reference program's by a relative error of at most 0.0003.
Values sent between devices are 32-bit elements; how exact they have to be, the bound alone decides.
No kernel may reach another device: no remote copies, remote signals or barrier semaphores. Data moves between devices by JAX's collectives and lax.ppermute only.
A program may use at most 128 MiB of HBM per device.

```python
import math
import jax
import jax.numpy as jnp
from jax import lax

BR = 1024
BC = 1024
K = 256
ROUNDS = 3
N_ROW = 32
N_COL = 4


def draw_counts(key, part):
    key = jax.random.fold_in(key, 7)
    first, second, third = jax.random.split(key, 3)
    shape = (ROUNDS, N_ROW * BR, N_COL * BC)
    livers = jax.random.randint(first, shape, 0, 3)
    levels = jax.random.randint(second, shape, 1, 9)
    upper = jnp.left_shift(jnp.ones(shape, jnp.int32), levels.astype(jnp.int32))
    values = jax.random.randint(third, shape, 1, upper)
    return jnp.where(livers > 0, values, 0).astype(jnp.int32)


def level_of(own_key, extent, cuts, least, top_value):
    level = 1.0
    for position, shards_of in cuts:
        steps = jax.random.uniform(jax.random.fold_in(jax.random.fold_in(own_key, 6), position), (shards_of,), jnp.float32, least / len(cuts), top_value / len(cuts))
        level = level * jnp.repeat(jnp.exp(steps), extent[position] // shards_of).reshape((-1,) + (1,) * (len(extent) - 1 - position))
    return level


def gaussian(rng, dims, spread, limit, pieces=(), held_as=jnp.bfloat16):
    values = spread * jax.random.normal(rng, dims, jnp.float32)
    if pieces:
        values = values * level_of(rng, dims, pieces, -0.22, 0.18)
    return jnp.clip(values, -limit, limit).astype(held_as)


def setup_inputs(seed: int = 0) -> dict:
    arg_keys = jax.random.split(jax.random.key(seed), 8)
    return {
        "counts": draw_counts(jax.random.fold_in(arg_keys[7], 71), 0),
        "row_embed": gaussian(arg_keys[1], (N_ROW * BR, K), 0.3, 1.5, ((0, 32),), jnp.float32),
        "row_accum": jnp.clip(jnp.exp(math.log(4.0) - 2.0794415 * jax.random.uniform(arg_keys[2], (N_ROW * BR, K), jnp.float32) ** level_of(arg_keys[2], (N_ROW * BR, K), ((0, 32),), -0.2, 0.2)), 0.5, 4.0),
        "col_embed": gaussian(arg_keys[3], (N_COL * BC, K), 0.3, 1.5, ((0, 4),), jnp.float32),
        "col_accum": jnp.clip(jnp.exp(math.log(4.0) - 2.0794415 * jax.random.uniform(arg_keys[4], (N_COL * BC, K), jnp.float32) ** level_of(arg_keys[4], (N_COL * BC, K), ((0, 4),), -0.2, 0.2)), 0.5, 4.0),
        "row_log": gaussian(arg_keys[5], (N_ROW * BR,), 1.0, 4.0, ((0, 32),), jnp.float32),
        "col_log": gaussian(arg_keys[6], (N_COL * BC,), 1.0, 4.0, ((0, 4),), jnp.float32),
    }


highest = lax.Precision.HIGHEST
learn_rate = 0.5

def swivel_residual(block, row_vecs, col_vecs, row_bias, col_bias):
    values = block.astype(jnp.float32)
    scores = jnp.dot(row_vecs, col_vecs.T, precision=highest, preferred_element_type=jnp.float32)
    base = -(row_bias[:, None] + col_bias[None, :])
    target = jnp.log(jnp.maximum(values, 1.0)) + base
    confidence = 0.1 + 0.25 * jnp.sqrt(values)
    return jnp.where(block > 0, confidence * (scores - target), jax.nn.sigmoid(scores - base))

def reference(counts, row_embed, row_accum, col_embed, col_accum, row_log, col_log):
    rows_all = row_embed.reshape(N_ROW, BR, K)
    rsum_all = row_accum.reshape(N_ROW, BR, K)
    rlog_all = row_log.reshape(N_ROW, BR)
    cols_all, csum_all, clog_all = (col_embed, col_accum, col_log)
    for turn in range(ROUNDS):
        if turn > 0:
            cols_all = jnp.roll(cols_all, BC, axis=0)
            csum_all = jnp.roll(csum_all, BC, axis=0)
            clog_all = jnp.roll(clog_all, BC, axis=0)
        blocks = counts[turn].reshape(N_ROW, BR, N_COL * BC)

        def one_block(carry, inputs, cols_all=cols_all, clog_all=clog_all):
            block, row_vecs, row_sums, row_bias = inputs
            residual = swivel_residual(block, row_vecs, cols_all, row_bias, clog_all)
            row_grad = jnp.dot(residual, cols_all, precision=highest, preferred_element_type=jnp.float32) / math.sqrt(N_COL * BC)
            new_sums = row_sums + row_grad * row_grad
            new_rows = row_vecs - learn_rate * row_grad / jnp.sqrt(new_sums)
            carry = carry + lax.dot_general(residual, row_vecs, (((0,), (0,)), ((), ())), precision=highest, preferred_element_type=jnp.float32)
            return (carry, (new_rows, new_sums))
        start = jnp.zeros((N_COL * BC, K), jnp.float32)
        product, (rows_all, rsum_all) = lax.scan(one_block, start, (blocks, rows_all, rsum_all, rlog_all))
        col_grad = product / math.sqrt(N_ROW * BR)
        csum_all = csum_all + col_grad * col_grad
        cols_all = cols_all - learn_rate * col_grad / jnp.sqrt(csum_all)
    return (rows_all.reshape(N_ROW * BR, K), rsum_all.reshape(N_ROW * BR, K), cols_all, csum_all)
```

```python
import math

import jax
import jax.numpy as jnp
from jax import lax
from jax.sharding import PartitionSpec as P

high = lax.Precision.HIGH
learn_rate = 0.5


def col_shift(block):
    n = lax.axis_size("col")
    return lax.ppermute(block, "col", [(i, (i + 1) % n) for i in range(n)])


def core_swap(block):
    n = lax.axis_size("col")
    return lax.ppermute(block, "col", [(i, i ^ 1) for i in range(n)])


def chip_swap(block):
    n = lax.axis_size("col")
    return lax.ppermute(block, "col", [(i, i ^ 2) for i in range(n)])


def swivel_residual(block, row_vecs, col_vecs, row_bias, col_bias):
    values = block.astype(jnp.float32)
    scores = jnp.dot(row_vecs, col_vecs.T, precision=high, preferred_element_type=jnp.float32)
    base = -(row_bias[:, None] + col_bias[None, :])
    target = jnp.log(jnp.maximum(values, 1.0)) + base
    confidence = 0.1 + 0.25 * jnp.sqrt(values)
    return jnp.where(block > 0, confidence * (scores - target), jax.nn.sigmoid(scores - base))


def adagrad(vecs, sums, grad):
    new_sums = sums + grad * grad
    return (vecs - learn_rate * grad / jnp.sqrt(new_sums), new_sums)


def row_sum(part):
    core = lax.axis_index("col") % 2
    half = part.shape[0] // 2
    halves = part.reshape(2, half, part.shape[1])
    mine = lax.dynamic_index_in_dim(halves, core, 0, keepdims=False)
    other = lax.dynamic_index_in_dim(halves, 1 - core, 0, keepdims=False)
    mine = mine + core_swap(other)
    mine = mine + chip_swap(mine)
    other = core_swap(mine)
    first = jnp.where(core == 0, mine, other)
    second = jnp.where(core == 0, other, mine)
    return jnp.concatenate([first, second], axis=0)


def row_gathered(piece):
    n = lax.axis_size("row")
    wide = jnp.broadcast_to(piece[None], (n,) + piece.shape)
    return lax.all_to_all(wide, "row", 0, 0).reshape(n * piece.shape[0], piece.shape[1])


def shards(counts, row_embed, row_accum, col_embed, col_accum, row_log, col_log):
    row_vecs, row_sums, row_bias = (row_embed, row_accum, row_log)
    col_vecs, col_bias = (col_embed, col_log)
    n_row = lax.axis_size("row")
    n_col = lax.axis_size("col")
    row_scale = math.sqrt(n_col * col_vecs.shape[0])
    col_scale = math.sqrt(n_row * row_vecs.shape[0])
    size = col_vecs.shape[0] // n_row
    me = lax.axis_index("row")
    piece = lax.dynamic_slice_in_dim(col_vecs, me * size, size, 0)
    piece_sums = lax.dynamic_slice_in_dim(col_accum, me * size, size, 0)
    turns = counts.shape[0]
    for turn in range(turns):
        residual = swivel_residual(counts[turn], row_vecs, col_vecs, row_bias, col_bias)
        product = lax.dot_general(
            residual,
            row_vecs,
            (((0,), (0,)), ((), ())),
            precision=high,
            preferred_element_type=jnp.float32,
        )
        row_part = jnp.dot(residual, col_vecs, precision=high, preferred_element_type=jnp.float32)
        row_total = row_sum(row_part)
        terms = lax.all_to_all(product.reshape(n_row, size, -1), "row", 0, 0)
        piece, piece_sums = adagrad(piece, piece_sums, jnp.sum(terms, axis=0) / col_scale)
        if turn < turns - 1:
            piece, piece_sums, col_bias = col_shift((piece, piece_sums, col_bias))
        col_vecs = row_gathered(piece)
        row_vecs, row_sums = adagrad(row_vecs, row_sums, row_total / row_scale)
    return (row_vecs, row_sums, col_vecs, row_gathered(piece_sums))


def solution(mesh):
    return jax.shard_map(
        shards,
        mesh=mesh,
        in_specs=(
            P(None, "row", "col"),
            P("row", None),
            P("row", None),
            P("col", None),
            P("col", None),
            P("row"),
            P("col"),
        ),
        out_specs=(P("row", None), P("row", None), P("col", None), P("col", None)),
        check_vma=False,
    )
```

```python
import functools
import math

import jax
import jax.numpy as jnp
from jax import lax
from jax.experimental import pallas as pl
from jax.experimental.pallas import tpu as pltpu
from jax.sharding import Mesh, PartitionSpec as P

learn_rate = 0.5
f32 = jnp.float32
bf16 = jnp.bfloat16
tile = 256

NN = (((1,), (0,)), ((), ()))
NT = (((1,), (1,)), ((), ()))
TN = (((0,), (0,)), ((), ()))


def halves(v):
    high = v.astype(bf16)
    return high, (v - high.astype(f32)).astype(bf16)


def dot3(a, b, dims):
    def one(x, y):
        return lax.dot_general(x, y, dims, preferred_element_type=f32)

    return one(a[0], b[0]) + (one(a[0], b[1]) + one(a[1], b[0]))


def residual_kernel(
    block_ref, row_ref, colt_ref, row_bias_ref, col_bias_ref,
    product_ref, high_ref, low_ref,
    row_high, row_low, rowt_high, rowt_low, bias,
):
    rows = row_ref.shape[0]

    @pl.when(pl.program_id(0) == 0)
    def _():
        for t in range(rows // tile):
            part = pl.ds(t * tile, tile)
            high, low = halves(row_ref[part, :])
            row_high[part, :] = high
            row_low[part, :] = low
            rowt_high[:, part] = high.T
            rowt_low[:, part] = low.T
        for t in range(rows // 128):
            bias[pl.ds(t * 128, 128), :] = jnp.broadcast_to(row_bias_ref[t:t + 1, :], (128, 128)).T

    cols = halves(colt_ref[...])
    col_bias = col_bias_ref[...]
    total = None
    for t in range(rows // tile):
        part = pl.ds(t * tile, tile)
        scores = dot3((row_high[part, :], row_low[part, :]), cols, NN)
        row_bias = bias[part, :]
        shifted = scores + (jnp.concatenate([row_bias] * (tile // 128), axis=1) + col_bias)
        block = block_ref[0, part, :]
        values = jnp.maximum(block.astype(f32), 1.0)
        confidence = 0.1 + 0.25 * (values * lax.rsqrt(values))
        seen = confidence * (shifted - jnp.log(values))
        unseen = 0.5 + 0.5 * jnp.tanh(0.5 * shifted)
        high, low = halves(jnp.where(block > 0, seen, unseen))
        high_ref[part, :] = high
        low_ref[part, :] = low
        term = dot3((rowt_high[:, part], rowt_low[:, part]), (high, low), NN)
        total = term if total is None else total + term
    product_ref[...] = total


def residual_and_product(turn, counts, row_vecs, colt, row_bias, col_bias):
    _, rows, cols = counts.shape
    k = row_vecs.shape[1]
    return pl.pallas_call(
        residual_kernel,
        grid=(cols // tile,),
        in_specs=[
            pl.BlockSpec((1, rows, tile), lambda c: (turn, 0, c)),
            pl.BlockSpec((rows, k), lambda c: (0, 0)),
            pl.BlockSpec((k, tile), lambda c: (0, c)),
            pl.BlockSpec((rows // 128, 128), lambda c: (0, 0)),
            pl.BlockSpec((1, tile), lambda c: (0, c)),
        ],
        out_specs=[
            pl.BlockSpec((k, tile), lambda c: (0, c)),
            pl.BlockSpec((rows, tile), lambda c: (0, c)),
            pl.BlockSpec((rows, tile), lambda c: (0, c)),
        ],
        out_shape=[
            jax.ShapeDtypeStruct((k, cols), f32),
            jax.ShapeDtypeStruct((rows, cols), bf16),
            jax.ShapeDtypeStruct((rows, cols), bf16),
        ],
        scratch_shapes=[
            pltpu.VMEM((rows, k), bf16),
            pltpu.VMEM((rows, k), bf16),
            pltpu.VMEM((k, rows), bf16),
            pltpu.VMEM((k, rows), bf16),
            pltpu.VMEM((rows, 128), f32),
        ],
        compiler_params=pltpu.CompilerParams(vmem_limit_bytes=40 * 2**20),
        cost_estimate=pl.CostEstimate(
            flops=12 * rows * cols * k, bytes_accessed=9 * rows * cols, transcendentals=3 * rows * cols
        ),
        name="residual",
    )(counts, row_vecs, colt, row_bias, col_bias)


def row_part_kernel(high_ref, low_ref, colt_ref, out_ref, col_high, col_low):
    @pl.when(pl.program_id(0) == 0)
    def _():
        high, low = halves(colt_ref[...])
        col_high[...] = high
        col_low[...] = low

    out_ref[...] = dot3((high_ref[...], low_ref[...]), (col_high[...], col_low[...]), NT)


def row_part_of(high, low, colt):
    rows, cols = high.shape
    k = colt.shape[0]
    return pl.pallas_call(
        row_part_kernel,
        grid=(rows // tile,),
        in_specs=[
            pl.BlockSpec((tile, cols), lambda r: (r, 0)),
            pl.BlockSpec((tile, cols), lambda r: (r, 0)),
            pl.BlockSpec((k, cols), lambda r: (0, 0)),
        ],
        out_specs=pl.BlockSpec((tile, k), lambda r: (r, 0)),
        out_shape=jax.ShapeDtypeStruct((rows, k), f32),
        scratch_shapes=[pltpu.VMEM((k, cols), bf16), pltpu.VMEM((k, cols), bf16)],
        compiler_params=pltpu.CompilerParams(vmem_limit_bytes=24 * 2**20),
        cost_estimate=pl.CostEstimate(
            flops=6 * rows * cols * k, bytes_accessed=4 * rows * cols, transcendentals=0
        ),
        name="row_part",
    )(high, low, colt)


def adagrad(vecs, sums, grad):
    new_sums = sums + grad * grad
    return (vecs - learn_rate * grad / jnp.sqrt(new_sums), new_sums)


def swap(block, axis):
    n = lax.axis_size(axis)
    return lax.ppermute(block, axis, [(i, i ^ 1) for i in range(n)])


def to_next_place(block):
    chips, cores = lax.axis_size("chip"), lax.axis_size("core")
    n = chips * cores
    return lax.ppermute(block, ("chip", "core"), [(i, (i + 1) % n) for i in range(n)])


def to_next_place_and_far(block):
    chips, cores = lax.axis_size("chip"), lax.axis_size("core")
    n = chips * cores
    route = [(h * n + i, (1 - h) * n + (i + 1) % n) for h in range(2) for i in range(n)]
    return lax.ppermute(block, ("far", "chip", "core"), route)


def row_sum(part):
    core = lax.axis_index("core")
    half = part.shape[0] // 2
    two = part.reshape(2, half, part.shape[1])
    mine = lax.dynamic_index_in_dim(two, core, 0, keepdims=False)
    other = lax.dynamic_index_in_dim(two, 1 - core, 0, keepdims=False)
    mine = mine + swap(other, "core")
    mine = mine + swap(mine, "chip")
    other = swap(mine, "core")
    first = jnp.where(core == 0, mine, other)
    second = jnp.where(core == 0, other, mine)
    return jnp.concatenate([first, second], axis=0)


plane = ("x", "z")


def gathered(piece):
    n = lax.axis_size("x") * lax.axis_size("z")
    wide = jnp.broadcast_to(piece[None], (n,) + piece.shape)
    return lax.all_to_all(wide, plane, 0, 0)


def shards(counts, row_embed, row_accum, col_embed, col_accum, row_log, col_log):
    row_vecs, row_sums = (row_embed, row_accum)
    colt = col_embed.T
    colt_sums = col_accum.T
    row_bias = row_log.reshape(-1, 128)
    col_bias = col_log.reshape(1, -1)
    n_plane = lax.axis_size("x") * lax.axis_size("z")
    n_row = n_plane * lax.axis_size("far")
    n_col = lax.axis_size("chip") * lax.axis_size("core")
    row_scale = math.sqrt(n_col * col_embed.shape[0])
    col_scale = math.sqrt(n_row * row_embed.shape[0])
    k, cols = colt.shape
    size = k // n_plane
    me = lax.axis_index("x") * lax.axis_size("z") + lax.axis_index("z")
    piece = lax.dynamic_slice_in_dim(colt, me * size, size, 0)
    piece_sums = lax.dynamic_slice_in_dim(colt_sums, me * size, size, 0)
    turns = counts.shape[0]
    for turn in range(turns):
        product, high, low = residual_and_product(turn, counts, row_vecs, colt, row_bias, col_bias)
        terms = lax.all_to_all(product.reshape(n_plane, size, cols), plane, 0, 0)
        row_total = row_sum(row_part_of(high, low, colt))
        total = jnp.sum(terms, axis=0)
        if turn < turns - 1:
            piece, piece_sums, col_bias = to_next_place((piece, piece_sums, col_bias))
            total = to_next_place(total) + to_next_place_and_far(total)
        else:
            total = total + swap(total, "far")
        piece, piece_sums = adagrad(piece, piece_sums, total / col_scale)
        if turn < turns - 1:
            colt = gathered(piece).reshape(k, cols)
        row_vecs, row_sums = adagrad(row_vecs, row_sums, row_total / row_scale)
    both = gathered(jnp.stack([piece, piece_sums]))
    return (row_vecs, row_sums, both[:, 0].reshape(k, cols).T, both[:, 1].reshape(k, cols).T)


def solution(mesh):
    fine = Mesh(mesh.devices.reshape(4, 4, 2, 2, 2), ("x", "z", "far", "chip", "core"))
    row = ("x", "z", "far")
    col = ("chip", "core")
    return jax.shard_map(
        shards,
        mesh=fine,
        in_specs=(
            P(None, row, col),
            P(row, None),
            P(row, None),
            P(col, None),
            P(col, None),
            P(row),
            P(col),
        ),
        out_specs=(P(row, None), P(row, None), P(col, None), P(col, None)),
        check_vma=False,
    )
```

```python
import functools
import math

import jax
import jax.numpy as jnp
from jax import lax
from jax.experimental import pallas as pl
from jax.experimental.pallas import tpu as pltpu
from jax.sharding import Mesh, PartitionSpec as P

learn_rate = 0.5
f32 = jnp.float32
bf16 = jnp.bfloat16
tile = 256
vmem_limit = 50 * 2**20
vmem_most = 50 * 2**20
vmem_small = 8 * 2**20
cross = 1

NN = (((1,), (0,)), ((), ()))
NT = (((1,), (1,)), ((), ()))
TN = (((0,), (0,)), ((), ()))


def parts(v, n):
    out = []
    for _ in range(n - 1):
        out.append(v.astype(bf16))
        v = v - out[-1].astype(f32)
    return out + [v.astype(bf16)]


def dot(a, b, dims):
    return lax.dot_general(a, b, dims, preferred_element_type=f32)


def folded(v, n):
    size = v.shape[0] // n
    total = v[(n - 1) * size:]
    for t in reversed(range(n - 1)):
        total = total + v[t * size:(t + 1) * size]
    return total


def residual_kernel(
    first, turn, counts_ref, row_in, col_in, row_bias_in, state_in,
    product_out, residual_out,
    row_ref, col_ref, row_bias_ref, col_bias_ref, product_ref,
    row_parts, rowt_parts, bias, scores, block_ref, residual_ref, sems, block_sems, residual_sems,
):
    rows, k = row_ref.shape
    cols = col_bias_ref.shape[1]
    loads = [
        pltpu.make_async_copy(source, target, sems.at[n])
        for n, (source, target) in enumerate(
            ((row_in, row_ref), (col_in, col_ref), (row_bias_in, row_bias_ref), (state_in.at[pl.ds(state_in.shape[0] - 8, 8)], col_bias_ref))
        )
    ]
    for load in loads:
        load.start()
    spans = [pl.ds(t * tile, tile) for t in range(rows // tile)]
    fetches = [
        pltpu.make_async_copy(counts_ref.at[turn, span, :], block_ref.at[span, :], block_sems.at[t])
        for t, span in enumerate(spans)
    ]
    stores = [
        pltpu.make_async_copy(residual_ref.at[span, :], residual_out.at[span, :], residual_sems.at[t])
        for t, span in enumerate(spans)
    ]
    for fetch in fetches:
        fetch.start()
    loads[0].wait()
    for t, span in enumerate(spans):
        for n, v in enumerate(parts(row_ref[span, :], 3)):
            if n < 2:
                row_parts[pl.ds(n * rows + t * tile, tile), :] = v
            rowt_parts[pl.ds(n * k, k), span] = v.T
    loads[2].wait()
    for t in range(rows // 128):
        bias[pl.ds(t * 128, 128), :] = jnp.broadcast_to(row_bias_ref[t:t + 1, :], (128, 128)).T
    loads[1].wait()
    loads[3].wait()
    col_high, col_low = parts(col_ref[...], 2)
    dims = NT if first else NN
    scores[...] = folded(dot(row_parts[...], col_high, dims), 2) + dot(row_parts[:rows, :], col_low, dims)
    col_bias = col_bias_ref[:1, :]
    total = None
    for t, span in enumerate(spans):
        row_bias = jnp.concatenate([bias[span, :]] * (cols // 128), axis=1)
        shifted = scores[span, :] + (row_bias + col_bias)
        fetches[t].wait()
        block = block_ref[span, :]
        values = jnp.maximum(block.astype(f32), 1.0)
        confidence = 0.1 + 0.25 * (values * lax.rsqrt(values))
        seen = confidence * (shifted - jnp.log(values))
        unseen = 0.5 + 0.5 * jnp.tanh(0.5 * shifted)
        residual = jnp.where(block > 0, seen, unseen)
        residual_ref[span, :] = residual
        stores[t].start()
        high, low = parts(residual, 2)
        term = folded(dot(rowt_parts[:cross * k, span], low, NN), cross)
        term = term + folded(dot(rowt_parts[:, span], high, NN), 3)
        total = term if total is None else total + term
    product_ref[...] = total
    out = pltpu.make_async_copy(product_ref, product_out, sems.at[0])
    out.start()
    for store in stores:
        store.wait()
    out.wait()


def residual_and_product(first, turn, counts, row_vecs, col_vecs, row_bias, state):
    _, rows, cols = counts.shape
    k = row_vecs.shape[1]
    steps = rows // tile
    far = pl.BlockSpec(memory_space=pltpu.HBM)
    return pl.pallas_call(
        functools.partial(residual_kernel, first, turn),
        in_specs=[far] * 5,
        out_specs=[far] * 2,
        out_shape=[
            jax.ShapeDtypeStruct((k, cols), f32),
            jax.ShapeDtypeStruct((rows, cols), f32),
        ],
        scratch_shapes=[
            pltpu.VMEM((rows, k), f32),
            pltpu.VMEM(col_vecs.shape, f32),
            pltpu.VMEM(row_bias.shape, f32),
            pltpu.VMEM((8, cols), f32),
            pltpu.VMEM((k, cols), f32),
            pltpu.VMEM((2 * rows, k), bf16),
            pltpu.VMEM((3 * k, rows), bf16),
            pltpu.VMEM((rows, 128), f32),
            pltpu.VMEM((rows, cols), f32),
            pltpu.VMEM((rows, cols), jnp.int32),
            pltpu.VMEM((rows, cols), f32),
            pltpu.SemaphoreType.DMA((4,)),
            pltpu.SemaphoreType.DMA((steps,)),
            pltpu.SemaphoreType.DMA((steps,)),
        ],
        compiler_params=pltpu.CompilerParams(vmem_limit_bytes=vmem_most),
        cost_estimate=pl.CostEstimate(flops=0, bytes_accessed=0, transcendentals=0),
        name="residual",
    )(counts, row_vecs, col_vecs, row_bias, state)


def row_part_kernel(first, half_ref, residual_ref, col_ref, out_ref, col_parts):
    @pl.when(pl.program_id(0) == 0)
    def _():
        for n, v in enumerate(parts(col_ref[...], 3)):
            col_parts[n] = v

    dims = NN if first else NT
    high, low = parts(residual_ref[...], 2)
    total = dot(high, col_parts[2], dims)
    for n in reversed(range(cross)):
        total = total + dot(low, col_parts[n], dims)
    for n in (1, 0):
        total = total + dot(high, col_parts[n], dims)
    out_ref[...] = total


def row_part_of(first, half, residual, col_vecs):
    rows, cols = residual.shape
    k = col_vecs.size // cols
    steps = rows // 2 // tile
    return pl.pallas_call(
        functools.partial(row_part_kernel, first),
        grid_spec=pltpu.PrefetchScalarGridSpec(
            num_scalar_prefetch=1,
            grid=(steps,),
            in_specs=[
                pl.BlockSpec((tile, cols), lambda r, half: (half[0] * steps + r, 0)),
                pl.BlockSpec(col_vecs.shape, lambda r, half: (0, 0)),
            ],
            out_specs=pl.BlockSpec((tile, k), lambda r, half: (r, 0)),
            scratch_shapes=[pltpu.VMEM((3,) + col_vecs.shape, bf16)],
        ),
        out_shape=jax.ShapeDtypeStruct((rows // 2, k), f32),
        compiler_params=pltpu.CompilerParams(vmem_limit_bytes=vmem_limit),
        cost_estimate=pl.CostEstimate(flops=0, bytes_accessed=0, transcendentals=0),
        name="row_part",
    )(jnp.full((1,), half, jnp.int32), residual, col_vecs)


def adagrad(vecs, sums, grad):
    new_sums = sums + grad * grad
    return (vecs - learn_rate * grad / jnp.sqrt(new_sums), new_sums)


def swap(block, axis):
    n = lax.axis_size(axis)
    return lax.ppermute(block, axis, [(i, i ^ 1) for i in range(n)])


def to_next_place(block):
    chips, cores = lax.axis_size("chip"), lax.axis_size("core")
    n = chips * cores
    return lax.ppermute(block, ("chip", "core"), [(i, (i + 1) % n) for i in range(n)])


def to_next_place_and_far(block):
    chips, cores = lax.axis_size("chip"), lax.axis_size("core")
    n = chips * cores
    route = [(h * n + i, (1 - h) * n + (i + 1) % n) for h in range(2) for i in range(n)]
    return lax.ppermute(block, ("far", "chip", "core"), route)


plane = ("x", "z")


def update_kernel(scale, copied, here_ref, there_ref, state_ref, wide_out, state_out, sems):
    size = here_ref.shape[0]
    grad = (here_ref[...] + there_ref[...]) / scale
    vecs, sums = adagrad(state_ref[:size, :], state_ref[size:2 * size, :], grad)
    state_out[:size, :] = vecs
    state_out[size:2 * size, :] = sums
    state_out[2 * size:, :] = state_ref[2 * size:, :]
    copies = [
        pltpu.make_async_copy(state_out.at[pl.ds(0, copied * size)], wide_out.at[n], sems.at[n])
        for n in range(wide_out.shape[0])
    ]
    for copy in copies:
        copy.start()
    for copy in copies:
        copy.wait()


def updated(scale, copies, copied, here, there, state):
    size, cols = here.shape
    near = pl.BlockSpec(memory_space=pltpu.VMEM)
    return pl.pallas_call(
        functools.partial(update_kernel, scale, copied),
        in_specs=[near] * 3,
        out_specs=[pl.BlockSpec(memory_space=pltpu.HBM), near],
        out_shape=[
            jax.ShapeDtypeStruct((copies, copied * size, cols), f32),
            jax.ShapeDtypeStruct(state.shape, f32),
        ],
        scratch_shapes=[pltpu.SemaphoreType.DMA((copies,))],
        compiler_params=pltpu.CompilerParams(vmem_limit_bytes=vmem_small),
        name="update",
    )(here, there, state)


def row_update_kernel(scale, core_ref, mine_ref, other_ref, vecs_ref, sums_ref, vecs_out, sums_out):
    half = mine_ref.shape[0]
    for ref, n in ((mine_ref, core_ref[0]), (other_ref, 1 - core_ref[0])):
        span = pl.ds(pl.multiple_of(n * half, half), half)
        vecs, sums = adagrad(vecs_ref[span, :], sums_ref[span, :], ref[...] / scale)
        vecs_out[span, :] = vecs
        sums_out[span, :] = sums


def row_updated(scale, core, mine, other, vecs, sums):
    near = pl.BlockSpec(memory_space=pltpu.VMEM)
    return pl.pallas_call(
        functools.partial(row_update_kernel, scale),
        in_specs=[pl.BlockSpec(memory_space=pltpu.SMEM)] + [near] * 4,
        out_specs=[near] * 2,
        out_shape=[jax.ShapeDtypeStruct(vecs.shape, f32)] * 2,
        compiler_params=pltpu.CompilerParams(vmem_limit_bytes=2 * vmem_small),
        cost_estimate=pl.CostEstimate(flops=0, bytes_accessed=0, transcendentals=0),
        name="row_update",
    )(jnp.full((1,), core, jnp.int32), mine, other, vecs, sums)


def upright_kernel(spread_ref, vecs_ref, sums_ref):
    n, both, cols = spread_ref.shape
    size = both // 2
    vecs_ref[...] = spread_ref[:, :size].reshape(n * size, cols).T
    sums_ref[...] = spread_ref[:, size:].reshape(n * size, cols).T


def upright(spread):
    n, both, cols = spread.shape
    k = n * both // 2
    wide = pl.BlockSpec((tile, k), lambda c: (c, 0))
    like = jax.ShapeDtypeStruct((cols, k), f32)
    return pl.pallas_call(
        upright_kernel,
        grid=(cols // tile,),
        in_specs=[pl.BlockSpec((n, both, tile), lambda c: (0, 0, c))],
        out_specs=[wide, wide],
        out_shape=[like, like],
        compiler_params=pltpu.CompilerParams(vmem_limit_bytes=vmem_limit),
        name="upright",
    )(spread)


def shards(counts, row_embed, row_accum, col_embed, col_accum, row_log, col_log):
    row_vecs, row_sums = (row_embed, row_accum)
    col_vecs = col_embed
    row_bias = row_log.reshape(-1, 128)
    n_plane = lax.axis_size("x") * lax.axis_size("z")
    n_row = n_plane * lax.axis_size("far")
    n_col = lax.axis_size("chip") * lax.axis_size("core")
    row_scale = math.sqrt(n_col * col_embed.shape[0])
    col_scale = math.sqrt(n_row * row_embed.shape[0])
    cols, k = col_embed.shape
    size = k // n_plane
    me = lax.axis_index("x") * lax.axis_size("z") + lax.axis_index("z")
    core = lax.axis_index("core")
    state = jnp.concatenate(
        [lax.dynamic_slice_in_dim(v, me * size, size, 1).T for v in (col_embed, col_accum)]
        + [jnp.broadcast_to(col_log[None], (8, cols))],
        axis=0,
    )
    turns = counts.shape[0]
    for turn in range(turns):
        first, last = turn == 0, turn == turns - 1
        product, residual = residual_and_product(first, turn, counts, row_vecs, col_vecs, row_bias, state)
        terms = lax.all_to_all(product.reshape(n_plane, size, cols), plane, 0, 0)
        other = swap(row_part_of(first, 1 - core, residual, col_vecs), "core")
        mine = row_part_of(first, core, residual, col_vecs) + other
        if not last:
            state = to_next_place(state)
        terms, mine, state = lax.optimization_barrier((terms, mine, state))
        total = jnp.sum(terms, axis=0)
        if not last:
            here, there = to_next_place(total), to_next_place_and_far(total)
        else:
            here, there = total, swap(total, "far")
        here, there, mine = lax.optimization_barrier((here, there, mine))
        wide, state = updated(col_scale, n_plane, 2 if last else 1, here, there, state)
        spread = lax.all_to_all(wide, plane, 0, 0)
        mine = mine + swap(mine, "chip")
        if last:
            col_vecs, col_sums = upright(spread)
        else:
            col_vecs = spread.reshape(k, cols)
        row_vecs, row_sums = row_updated(row_scale, core, mine, swap(mine, "core"), row_vecs, row_sums)
    return (row_vecs, row_sums, col_vecs, col_sums)


def solution(mesh):
    fine = Mesh(mesh.devices.reshape(4, 4, 2, 2, 2), ("x", "z", "far", "chip", "core"))
    row = ("x", "z", "far")
    col = ("chip", "core")
    return jax.shard_map(
        shards,
        mesh=fine,
        in_specs=(
            P(None, row, col),
            P(row, None),
            P(row, None),
            P(col, None),
            P(col, None),
            P(row),
            P(col),
        ),
        out_specs=(P(row, None), P(row, None), P(col, None), P(col, None)),
        check_vma=False,
    )
```

```python
import functools
import math

import jax
import jax.numpy as jnp
from jax import lax
from jax.experimental import pallas as pl
from jax.experimental.pallas import tpu as pltpu
from jax.sharding import Mesh, PartitionSpec as P

learn_rate = 0.5
f32 = jnp.float32
bf16 = jnp.bfloat16
tile = 256
chunk = 512
vmem_limit = 50 * 2**20
vmem_most = 50 * 2**20
vmem_small = 8 * 2**20
cross = 1

NN = (((1,), (0,)), ((), ()))
NT = (((1,), (1,)), ((), ()))
TN = (((0,), (0,)), ((), ()))


def parts(v, n):
    out = []
    for _ in range(n - 1):
        out.append(v.astype(bf16))
        v = v - out[-1].astype(f32)
    return out + [v.astype(bf16)]


def dot(a, b, dims):
    return lax.dot_general(a, b, dims, preferred_element_type=f32)


def folded(v, n):
    size = v.shape[0] // n
    total = v[(n - 1) * size:]
    for t in reversed(range(n - 1)):
        total = total + v[t * size:(t + 1) * size]
    return total


def residual_kernel(
    first, turn, counts_ref, row_in, col_in, row_bias_in, state_in,
    product_out, residual_out,
    row_ref, col_ref, row_bias_ref, col_bias_ref, product_ref,
    row_parts, rowt_parts, bias, scores, block_ref, residual_ref, sems, block_sems, residual_sems,
):
    rows, k = row_ref.shape
    cols = col_bias_ref.shape[1]
    loads = [
        pltpu.make_async_copy(source, target, sems.at[n])
        for n, (source, target) in enumerate(
            ((row_in, row_ref), (col_in, col_ref), (row_bias_in, row_bias_ref), (state_in.at[pl.ds(state_in.shape[0] - 8, 8)], col_bias_ref))
        )
    ]
    for load in loads:
        load.start()
    spans = [pl.ds(t * chunk, chunk) for t in range(rows // chunk)]
    fetches = [
        pltpu.make_async_copy(counts_ref.at[turn, span, :], block_ref.at[span, :], block_sems.at[t])
        for t, span in enumerate(spans)
    ]
    stores = [
        pltpu.make_async_copy(residual_ref.at[span, :], residual_out.at[span, :], residual_sems.at[t])
        for t, span in enumerate(spans)
    ]
    for fetch in fetches:
        fetch.start()
    loads[0].wait()
    for t, span in enumerate(spans):
        for n, v in enumerate(parts(row_ref[span, :], 3)):
            if n < 2:
                row_parts[pl.ds(n * rows + t * chunk, chunk), :] = v
            rowt_parts[pl.ds(n * k, k), span] = v.T
    loads[2].wait()
    for t in range(rows // 128):
        bias[pl.ds(t * 128, 128), :] = jnp.broadcast_to(row_bias_ref[t:t + 1, :], (128, 128)).T
    loads[1].wait()
    loads[3].wait()
    col_high, col_low = parts(col_ref[...], 2)
    dims = NT if first else NN
    scores[...] = folded(dot(row_parts[...], col_high, dims), 2) + dot(row_parts[:rows, :], col_low, dims)
    col_bias = col_bias_ref[:1, :]
    total = None
    for t, span in enumerate(spans):
        row_bias = jnp.concatenate([bias[span, :]] * (cols // 128), axis=1)
        shifted = scores[span, :] + (row_bias + col_bias)
        fetches[t].wait()
        block = block_ref[span, :]
        values = jnp.maximum(block.astype(f32), 1.0)
        confidence = 0.1 + 0.25 * (values * lax.rsqrt(values))
        seen = confidence * (shifted - jnp.log(values))
        unseen = 0.5 + 0.5 * jnp.tanh(0.5 * shifted)
        residual = jnp.where(block > 0, seen, unseen)
        residual_ref[span, :] = residual
        stores[t].start()
        high, low = parts(residual, 2)
        term = folded(dot(rowt_parts[:cross * k, span], low, NN), cross)
        term = term + folded(dot(rowt_parts[:, span], high, NN), 3)
        total = term if total is None else total + term
    product_ref[...] = total
    out = pltpu.make_async_copy(product_ref, product_out, sems.at[0])
    out.start()
    for store in stores:
        store.wait()
    out.wait()


def residual_and_product(first, turn, counts, row_vecs, col_vecs, row_bias, state):
    _, rows, cols = counts.shape
    k = row_vecs.shape[1]
    steps = rows // chunk
    far = pl.BlockSpec(memory_space=pltpu.HBM)
    return pl.pallas_call(
        functools.partial(residual_kernel, first, turn),
        in_specs=[far] * 5,
        out_specs=[far] * 2,
        out_shape=[
            jax.ShapeDtypeStruct((k, cols), f32),
            jax.ShapeDtypeStruct((rows, cols), f32),
        ],
        scratch_shapes=[
            pltpu.VMEM((rows, k), f32),
            pltpu.VMEM(col_vecs.shape, f32),
            pltpu.VMEM(row_bias.shape, f32),
            pltpu.VMEM((8, cols), f32),
            pltpu.VMEM((k, cols), f32),
            pltpu.VMEM((2 * rows, k), bf16),
            pltpu.VMEM((3 * k, rows), bf16),
            pltpu.VMEM((rows, 128), f32),
            pltpu.VMEM((rows, cols), f32),
            pltpu.VMEM((rows, cols), jnp.int32),
            pltpu.VMEM((rows, cols), f32),
            pltpu.SemaphoreType.DMA((4,)),
            pltpu.SemaphoreType.DMA((steps,)),
            pltpu.SemaphoreType.DMA((steps,)),
        ],
        compiler_params=pltpu.CompilerParams(vmem_limit_bytes=vmem_most),
        cost_estimate=pl.CostEstimate(flops=0, bytes_accessed=0, transcendentals=0),
        name="residual",
    )(counts, row_vecs, col_vecs, row_bias, state)


def row_part_kernel(first, half_ref, residual_ref, col_ref, out_ref, col_parts):
    @pl.when(pl.program_id(0) == 0)
    def _():
        for n, v in enumerate(parts(col_ref[...], 3)):
            col_parts[n] = v

    dims = NN if first else NT
    high, low = parts(residual_ref[...], 2)
    total = dot(high, col_parts[2], dims)
    for n in reversed(range(cross)):
        total = total + dot(low, col_parts[n], dims)
    for n in (1, 0):
        total = total + dot(high, col_parts[n], dims)
    out_ref[...] = total


def row_part_of(first, half, residual, col_vecs):
    rows, cols = residual.shape
    k = col_vecs.size // cols
    steps = rows // 2 // tile
    return pl.pallas_call(
        functools.partial(row_part_kernel, first),
        grid_spec=pltpu.PrefetchScalarGridSpec(
            num_scalar_prefetch=1,
            grid=(steps,),
            in_specs=[
                pl.BlockSpec((tile, cols), lambda r, half: (half[0] * steps + r, 0)),
                pl.BlockSpec(col_vecs.shape, lambda r, half: (0, 0)),
            ],
            out_specs=pl.BlockSpec((tile, k), lambda r, half: (r, 0)),
            scratch_shapes=[pltpu.VMEM((3,) + col_vecs.shape, bf16)],
        ),
        out_shape=jax.ShapeDtypeStruct((rows // 2, k), f32),
        compiler_params=pltpu.CompilerParams(vmem_limit_bytes=vmem_limit),
        cost_estimate=pl.CostEstimate(flops=0, bytes_accessed=0, transcendentals=0),
        name="row_part",
    )(jnp.full((1,), half, jnp.int32), residual, col_vecs)


def adagrad(vecs, sums, grad):
    new_sums = sums + grad * grad
    return (vecs - learn_rate * grad / jnp.sqrt(new_sums), new_sums)


def swap(block, axis):
    n = lax.axis_size(axis)
    return lax.ppermute(block, axis, [(i, i ^ 1) for i in range(n)])


def to_next_place(block):
    chips, cores = lax.axis_size("chip"), lax.axis_size("core")
    n = chips * cores
    return lax.ppermute(block, ("chip", "core"), [(i, (i + 1) % n) for i in range(n)])


def to_next_place_and_far(block):
    chips, cores = lax.axis_size("chip"), lax.axis_size("core")
    n = chips * cores
    route = [(h * n + i, (1 - h) * n + (i + 1) % n) for h in range(2) for i in range(n)]
    return lax.ppermute(block, ("far", "chip", "core"), route)


plane = ("x", "z")


def update_kernel(scale, copied, here_ref, there_ref, state_ref, wide_out, state_out, sems):
    size = here_ref.shape[0]
    grad = (here_ref[...] + there_ref[...]) / scale
    vecs, sums = adagrad(state_ref[:size, :], state_ref[size:2 * size, :], grad)
    state_out[:size, :] = vecs
    state_out[size:2 * size, :] = sums
    state_out[2 * size:, :] = state_ref[2 * size:, :]
    copies = [
        pltpu.make_async_copy(state_out.at[pl.ds(0, copied * size)], wide_out.at[n], sems.at[n])
        for n in range(wide_out.shape[0])
    ]
    for copy in copies:
        copy.start()
    for copy in copies:
        copy.wait()


def updated(scale, copies, copied, here, there, state):
    size, cols = here.shape
    near = pl.BlockSpec(memory_space=pltpu.VMEM)
    return pl.pallas_call(
        functools.partial(update_kernel, scale, copied),
        in_specs=[near] * 3,
        out_specs=[pl.BlockSpec(memory_space=pltpu.HBM), near],
        out_shape=[
            jax.ShapeDtypeStruct((copies, copied * size, cols), f32),
            jax.ShapeDtypeStruct(state.shape, f32),
        ],
        scratch_shapes=[pltpu.SemaphoreType.DMA((copies,))],
        compiler_params=pltpu.CompilerParams(vmem_limit_bytes=vmem_small),
        name="update",
    )(here, there, state)


def row_update_kernel(scale, core_ref, mine_ref, other_ref, vecs_ref, sums_ref, vecs_out, sums_out):
    half = mine_ref.shape[0]
    for ref, n in ((mine_ref, core_ref[0]), (other_ref, 1 - core_ref[0])):
        span = pl.ds(pl.multiple_of(n * half, half), half)
        vecs, sums = adagrad(vecs_ref[span, :], sums_ref[span, :], ref[...] / scale)
        vecs_out[span, :] = vecs
        sums_out[span, :] = sums


def row_updated(scale, core, mine, other, vecs, sums):
    near = pl.BlockSpec(memory_space=pltpu.VMEM)
    return pl.pallas_call(
        functools.partial(row_update_kernel, scale),
        in_specs=[pl.BlockSpec(memory_space=pltpu.SMEM)] + [near] * 4,
        out_specs=[near] * 2,
        out_shape=[jax.ShapeDtypeStruct(vecs.shape, f32)] * 2,
        compiler_params=pltpu.CompilerParams(vmem_limit_bytes=2 * vmem_small),
        cost_estimate=pl.CostEstimate(flops=0, bytes_accessed=0, transcendentals=0),
        name="row_update",
    )(jnp.full((1,), core, jnp.int32), mine, other, vecs, sums)


def upright_kernel(spread_ref, vecs_ref, sums_ref):
    n, both, cols = spread_ref.shape
    size = both // 2
    vecs_ref[...] = spread_ref[:, :size].reshape(n * size, cols).T
    sums_ref[...] = spread_ref[:, size:].reshape(n * size, cols).T


def upright(spread):
    n, both, cols = spread.shape
    k = n * both // 2
    wide = pl.BlockSpec((tile, k), lambda c: (c, 0))
    like = jax.ShapeDtypeStruct((cols, k), f32)
    return pl.pallas_call(
        upright_kernel,
        grid=(cols // tile,),
        in_specs=[pl.BlockSpec((n, both, tile), lambda c: (0, 0, c))],
        out_specs=[wide, wide],
        out_shape=[like, like],
        compiler_params=pltpu.CompilerParams(vmem_limit_bytes=vmem_limit),
        name="upright",
    )(spread)


def shards(counts, row_embed, row_accum, col_embed, col_accum, row_log, col_log):
    row_vecs, row_sums = (row_embed, row_accum)
    col_vecs = col_embed
    row_bias = row_log.reshape(-1, 128)
    n_plane = lax.axis_size("x") * lax.axis_size("z")
    n_row = n_plane * lax.axis_size("far")
    n_col = lax.axis_size("chip") * lax.axis_size("core")
    row_scale = math.sqrt(n_col * col_embed.shape[0])
    col_scale = math.sqrt(n_row * row_embed.shape[0])
    cols, k = col_embed.shape
    size = k // n_plane
    me = lax.axis_index("x") * lax.axis_size("z") + lax.axis_index("z")
    core = lax.axis_index("core")
    state = jnp.concatenate(
        [lax.dynamic_slice_in_dim(v, me * size, size, 1).T for v in (col_embed, col_accum)]
        + [jnp.broadcast_to(col_log[None], (8, cols))],
        axis=0,
    )
    turns = counts.shape[0]
    for turn in range(turns):
        first, last = turn == 0, turn == turns - 1
        product, residual = residual_and_product(first, turn, counts, row_vecs, col_vecs, row_bias, state)
        terms = lax.all_to_all(product.reshape(n_plane, size, cols), plane, 0, 0)
        other = swap(row_part_of(first, 1 - core, residual, col_vecs), "core")
        mine = row_part_of(first, core, residual, col_vecs) + other
        if not last:
            state = to_next_place(state)
        terms, mine, state = lax.optimization_barrier((terms, mine, state))
        total = jnp.sum(terms, axis=0)
        if not last:
            here, there = to_next_place(total), to_next_place_and_far(total)
        else:
            here, there = total, swap(total, "far")
        here, there, mine = lax.optimization_barrier((here, there, mine))
        wide, state = updated(col_scale, n_plane, 2 if last else 1, here, there, state)
        spread = lax.all_to_all(wide, plane, 0, 0)
        mine = mine + swap(mine, "chip")
        if last:
            col_vecs, col_sums = upright(spread)
        else:
            col_vecs = spread.reshape(k, cols)
        row_vecs, row_sums = row_updated(row_scale, core, mine, swap(mine, "core"), row_vecs, row_sums)
    return (row_vecs, row_sums, col_vecs, col_sums)


def solution(mesh):
    fine = Mesh(mesh.devices.reshape(4, 4, 2, 2, 2), ("x", "z", "far", "chip", "core"))
    row = ("x", "z", "far")
    col = ("chip", "core")
    return jax.shard_map(
        shards,
        mesh=fine,
        in_specs=(
            P(None, row, col),
            P(row, None),
            P(row, None),
            P(col, None),
            P(col, None),
            P(row),
            P(col),
        ),
        out_specs=(P(row, None), P(row, None), P(col, None), P(col, None)),
        check_vma=False,
    )
```

```python
import functools
import math

import jax
import jax.numpy as jnp
from jax import lax
from jax.experimental import pallas as pl
from jax.experimental.pallas import tpu as pltpu
from jax.sharding import Mesh, PartitionSpec as P

learn_rate = 0.5
f32 = jnp.float32
bf16 = jnp.bfloat16
tile = 256
chunk = 512
vmem_limit = 50 * 2**20
vmem_most = 50 * 2**20
vmem_small = 8 * 2**20
cross = 1

NN = (((1,), (0,)), ((), ()))
NT = (((1,), (1,)), ((), ()))
TN = (((0,), (0,)), ((), ()))


def parts(v, n):
    out = []
    for _ in range(n - 1):
        out.append(v.astype(bf16))
        v = v - out[-1].astype(f32)
    return out + [v.astype(bf16)]


def dot(a, b, dims):
    return lax.dot_general(a, b, dims, preferred_element_type=f32)


def folded(v, n):
    size = v.shape[0] // n
    total = v[(n - 1) * size:]
    for t in reversed(range(n - 1)):
        total = total + v[t * size:(t + 1) * size]
    return total


def residual_kernel(
    first, turn, counts_ref, row_in, col_in, row_bias_in, state_in,
    product_out, residual_out,
    row_ref, col_ref, row_bias_ref, col_bias_ref, product_ref,
    row_parts, rowt_parts, bias, scores, block_ref, residual_ref, sems, block_sems, residual_sems,
):
    rows, k = row_ref.shape
    cols = col_bias_ref.shape[1]
    loads = [
        pltpu.make_async_copy(source, target, sems.at[n])
        for n, (source, target) in enumerate(
            ((row_in, row_ref), (col_in, col_ref), (row_bias_in, row_bias_ref), (state_in.at[pl.ds(state_in.shape[0] - 8, 8)], col_bias_ref))
        )
    ]
    for load in loads:
        load.start()
    spans = [pl.ds(t * chunk, chunk) for t in range(rows // chunk)]
    fetches = [
        pltpu.make_async_copy(counts_ref.at[turn, span, :], block_ref.at[span, :], block_sems.at[t])
        for t, span in enumerate(spans)
    ]
    stores = [
        pltpu.make_async_copy(residual_ref.at[span, :], residual_out.at[span, :], residual_sems.at[t])
        for t, span in enumerate(spans)
    ]
    for fetch in fetches:
        fetch.start()
    loads[0].wait()
    for t, span in enumerate(spans):
        for n, v in enumerate(parts(row_ref[span, :], 3)):
            if n < 2:
                row_parts[pl.ds(n * rows + t * chunk, chunk), :] = v
            rowt_parts[pl.ds(n * k, k), span] = v.T
    loads[2].wait()
    for t in range(rows // 128):
        bias[pl.ds(t * 128, 128), :] = jnp.broadcast_to(row_bias_ref[t:t + 1, :], (128, 128)).T
    loads[1].wait()
    loads[3].wait()
    col_high, col_low = parts(col_ref[...], 2)
    dims = NT if first else NN
    scores[...] = folded(dot(row_parts[...], col_high, dims), 2) + dot(row_parts[:rows, :], col_low, dims)
    col_bias = col_bias_ref[:1, :]
    total = None
    for t, span in enumerate(spans):
        row_bias = jnp.concatenate([bias[span, :]] * (cols // 128), axis=1)
        shifted = scores[span, :] + (row_bias + col_bias)
        fetches[t].wait()
        block = block_ref[span, :]
        values = jnp.maximum(block.astype(f32), 1.0)
        confidence = 0.1 + 0.25 * (values * lax.rsqrt(values))
        seen = confidence * (shifted - jnp.log(values))
        unseen = 0.5 + 0.5 * jnp.tanh(0.5 * shifted)
        residual = jnp.where(block > 0, seen, unseen)
        residual_ref[span, :] = residual
        stores[t].start()
        high, low = parts(residual, 2)
        term = folded(dot(rowt_parts[:cross * k, span], low, NN), cross)
        term = term + folded(dot(rowt_parts[:, span], high, NN), 3)
        total = term if total is None else total + term
    product_ref[...] = total
    out = pltpu.make_async_copy(product_ref, product_out, sems.at[0])
    out.start()
    for store in stores:
        store.wait()
    out.wait()


def residual_and_product(first, turn, counts, row_vecs, col_vecs, row_bias, state):
    _, rows, cols = counts.shape
    k = row_vecs.shape[1]
    steps = rows // chunk
    far = pl.BlockSpec(memory_space=pltpu.HBM)
    return pl.pallas_call(
        functools.partial(residual_kernel, first, turn),
        in_specs=[far] * 5,
        out_specs=[far] * 2,
        out_shape=[
            jax.ShapeDtypeStruct((k, cols), f32),
            jax.ShapeDtypeStruct((rows, cols), f32),
        ],
        scratch_shapes=[
            pltpu.VMEM((rows, k), f32),
            pltpu.VMEM(col_vecs.shape, f32),
            pltpu.VMEM(row_bias.shape, f32),
            pltpu.VMEM((8, cols), f32),
            pltpu.VMEM((k, cols), f32),
            pltpu.VMEM((2 * rows, k), bf16),
            pltpu.VMEM((3 * k, rows), bf16),
            pltpu.VMEM((rows, 128), f32),
            pltpu.VMEM((rows, cols), f32),
            pltpu.VMEM((rows, cols), jnp.int32),
            pltpu.VMEM((rows, cols), f32),
            pltpu.SemaphoreType.DMA((4,)),
            pltpu.SemaphoreType.DMA((steps,)),
            pltpu.SemaphoreType.DMA((steps,)),
        ],
        compiler_params=pltpu.CompilerParams(vmem_limit_bytes=vmem_most),
        cost_estimate=pl.CostEstimate(flops=0, bytes_accessed=0, transcendentals=0),
        name="residual",
    )(counts, row_vecs, col_vecs, row_bias, state)


def row_part_kernel(first, half_ref, residual_ref, col_ref, out_ref, col_parts):
    @pl.when(pl.program_id(0) == 0)
    def _():
        for n, v in enumerate(parts(col_ref[...], 3)):
            col_parts[n] = v

    dims = NN if first else NT
    high, low = parts(residual_ref[...], 2)
    total = dot(high, col_parts[2], dims)
    for n in reversed(range(cross)):
        total = total + dot(low, col_parts[n], dims)
    for n in (1, 0):
        total = total + dot(high, col_parts[n], dims)
    out_ref[...] = total


def row_part_of(first, half, residual, col_vecs):
    rows, cols = residual.shape
    k = col_vecs.size // cols
    steps = rows // 2 // tile
    return pl.pallas_call(
        functools.partial(row_part_kernel, first),
        grid_spec=pltpu.PrefetchScalarGridSpec(
            num_scalar_prefetch=1,
            grid=(steps,),
            in_specs=[
                pl.BlockSpec((tile, cols), lambda r, half: (half[0] * steps + r, 0)),
                pl.BlockSpec(col_vecs.shape, lambda r, half: (0, 0)),
            ],
            out_specs=pl.BlockSpec((tile, k), lambda r, half: (r, 0)),
            scratch_shapes=[pltpu.VMEM((3,) + col_vecs.shape, bf16)],
        ),
        out_shape=jax.ShapeDtypeStruct((rows // 2, k), f32),
        compiler_params=pltpu.CompilerParams(vmem_limit_bytes=vmem_limit),
        cost_estimate=pl.CostEstimate(flops=0, bytes_accessed=0, transcendentals=0),
        name="row_part",
    )(jnp.full((1,), half, jnp.int32), residual, col_vecs)


def adagrad(vecs, sums, grad):
    new_sums = sums + grad * grad
    return (vecs - learn_rate * grad / jnp.sqrt(new_sums), new_sums)


def swap(block, axis):
    n = lax.axis_size(axis)
    return lax.ppermute(block, axis, [(i, i ^ 1) for i in range(n)])


def to_next_place(block):
    chips, cores = lax.axis_size("chip"), lax.axis_size("core")
    n = chips * cores
    return lax.ppermute(block, ("chip", "core"), [(i, (i + 1) % n) for i in range(n)])


def to_next_place_and_far(block):
    chips, cores = lax.axis_size("chip"), lax.axis_size("core")
    n = chips * cores
    route = [(h * n + i, (1 - h) * n + (i + 1) % n) for h in range(2) for i in range(n)]
    return lax.ppermute(block, ("far", "chip", "core"), route)


plane = ("x", "z")


def update_kernel(scale, copied, here_ref, there_ref, state_ref, wide_out, state_out, sems):
    size = here_ref.shape[0]
    grad = (here_ref[...] + there_ref[...]) / scale
    vecs, sums = adagrad(state_ref[:size, :], state_ref[size:2 * size, :], grad)
    state_out[:size, :] = vecs
    state_out[size:2 * size, :] = sums
    state_out[2 * size:, :] = state_ref[2 * size:, :]
    copies = [
        pltpu.make_async_copy(state_out.at[pl.ds(0, copied * size)], wide_out.at[n], sems.at[n])
        for n in range(wide_out.shape[0])
    ]
    for copy in copies:
        copy.start()
    for copy in copies:
        copy.wait()


def updated(scale, copies, copied, here, there, state):
    size, cols = here.shape
    near = pl.BlockSpec(memory_space=pltpu.VMEM)
    return pl.pallas_call(
        functools.partial(update_kernel, scale, copied),
        in_specs=[near] * 3,
        out_specs=[pl.BlockSpec(memory_space=pltpu.HBM), near],
        out_shape=[
            jax.ShapeDtypeStruct((copies, copied * size, cols), f32),
            jax.ShapeDtypeStruct(state.shape, f32),
        ],
        scratch_shapes=[pltpu.SemaphoreType.DMA((copies,))],
        compiler_params=pltpu.CompilerParams(vmem_limit_bytes=vmem_small),
        name="update",
    )(here, there, state)


def sum_kernel(terms_ref, out_ref):
    total = terms_ref[0]
    for n in range(1, terms_ref.shape[0]):
        total = total + terms_ref[n]
    out_ref[...] = total


def summed(terms):
    n, size, cols = terms.shape
    wide = 2 * tile
    return pl.pallas_call(
        sum_kernel,
        grid=(cols // wide,),
        in_specs=[pl.BlockSpec((n, size, wide), lambda c: (0, 0, c))],
        out_specs=pl.BlockSpec((size, wide), lambda c: (0, c)),
        out_shape=jax.ShapeDtypeStruct((size, cols), f32),
        compiler_params=pltpu.CompilerParams(vmem_limit_bytes=vmem_small),
        name="sum",
    )(terms)


def row_update_kernel(scale, core_ref, mine_ref, other_ref, vecs_ref, sums_ref, vecs_out, sums_out):
    half = mine_ref.shape[0]
    for ref, n in ((mine_ref, core_ref[0]), (other_ref, 1 - core_ref[0])):
        span = pl.ds(pl.multiple_of(n * half, half), half)
        vecs, sums = adagrad(vecs_ref[span, :], sums_ref[span, :], ref[...] / scale)
        vecs_out[span, :] = vecs
        sums_out[span, :] = sums


def row_updated(scale, core, mine, other, vecs, sums):
    near = pl.BlockSpec(memory_space=pltpu.VMEM)
    return pl.pallas_call(
        functools.partial(row_update_kernel, scale),
        in_specs=[pl.BlockSpec(memory_space=pltpu.SMEM)] + [near] * 4,
        out_specs=[near] * 2,
        out_shape=[jax.ShapeDtypeStruct(vecs.shape, f32)] * 2,
        compiler_params=pltpu.CompilerParams(vmem_limit_bytes=2 * vmem_small),
        cost_estimate=pl.CostEstimate(flops=0, bytes_accessed=0, transcendentals=0),
        name="row_update",
    )(jnp.full((1,), core, jnp.int32), mine, other, vecs, sums)


def upright_kernel(spread_ref, vecs_ref, sums_ref):
    n, both, cols = spread_ref.shape
    size = both // 2
    vecs_ref[...] = spread_ref[:, :size].reshape(n * size, cols).T
    sums_ref[...] = spread_ref[:, size:].reshape(n * size, cols).T


def upright(spread):
    n, both, cols = spread.shape
    k = n * both // 2
    wide = pl.BlockSpec((tile, k), lambda c: (c, 0))
    like = jax.ShapeDtypeStruct((cols, k), f32)
    return pl.pallas_call(
        upright_kernel,
        grid=(cols // tile,),
        in_specs=[pl.BlockSpec((n, both, tile), lambda c: (0, 0, c))],
        out_specs=[wide, wide],
        out_shape=[like, like],
        compiler_params=pltpu.CompilerParams(vmem_limit_bytes=vmem_limit),
        name="upright",
    )(spread)


def shards(counts, row_embed, row_accum, col_embed, col_accum, row_log, col_log):
    row_vecs, row_sums = (row_embed, row_accum)
    col_vecs = col_embed
    row_bias = row_log.reshape(-1, 128)
    n_plane = lax.axis_size("x") * lax.axis_size("z")
    n_row = n_plane * lax.axis_size("far")
    n_col = lax.axis_size("chip") * lax.axis_size("core")
    row_scale = math.sqrt(n_col * col_embed.shape[0])
    col_scale = math.sqrt(n_row * row_embed.shape[0])
    cols, k = col_embed.shape
    size = k // n_plane
    me = lax.axis_index("x") * lax.axis_size("z") + lax.axis_index("z")
    core = lax.axis_index("core")
    state = jnp.concatenate(
        [lax.dynamic_slice_in_dim(v, me * size, size, 1).T for v in (col_embed, col_accum)]
        + [jnp.broadcast_to(col_log[None], (8, cols))],
        axis=0,
    )
    turns = counts.shape[0]
    for turn in range(turns):
        first, last = turn == 0, turn == turns - 1
        product, residual = residual_and_product(first, turn, counts, row_vecs, col_vecs, row_bias, state)
        terms = lax.all_to_all(product.reshape(n_plane, size, cols), plane, 0, 0)
        other = swap(row_part_of(first, 1 - core, residual, col_vecs), "core")
        mine = row_part_of(first, core, residual, col_vecs) + other
        if not last:
            state = to_next_place(state)
        terms, mine, state = lax.optimization_barrier((terms, mine, state))
        total = summed(terms)
        if not last:
            here, there = to_next_place(total), to_next_place_and_far(total)
        else:
            here, there = total, swap(total, "far")
        here, there, mine = lax.optimization_barrier((here, there, mine))
        wide, state = updated(col_scale, n_plane, 2 if last else 1, here, there, state)
        spread = lax.all_to_all(wide, plane, 0, 0)
        mine = mine + swap(mine, "chip")
        if last:
            col_vecs, col_sums = upright(spread)
        else:
            col_vecs = spread.reshape(k, cols)
        row_vecs, row_sums = row_updated(row_scale, core, mine, swap(mine, "core"), row_vecs, row_sums)
    return (row_vecs, row_sums, col_vecs, col_sums)


def solution(mesh):
    fine = Mesh(mesh.devices.reshape(4, 4, 2, 2, 2), ("x", "z", "far", "chip", "core"))
    row = ("x", "z", "far")
    col = ("chip", "core")
    return jax.shard_map(
        shards,
        mesh=fine,
        in_specs=(
            P(None, row, col),
            P(row, None),
            P(row, None),
            P(col, None),
            P(col, None),
            P(row),
            P(col),
        ),
        out_specs=(P(row, None), P(row, None), P(col, None), P(col, None)),
        check_vma=False,
    )
```
